32 devices in a mesh: row: 4 (over y, x), col: 2 (over core), layer: 4 (over z).
Axes of the slice: x: 2, y: 2, z: 4, core: 2. Of those that a mesh axis runs over, the one named last changes fastest.
Arguments:
- values: float32 [2048, 2048], P('row', ('layer', 'col')), may hold values from 0 to 2
- a_pattern: int32 [16, 16], P('row', ('layer', 'col')), may hold values from 0 to 1, as said below
- c_pattern: int32 [16, 16], P('row', ('layer', 'col')), may hold values 0 or 1
- prune_mask: int32 [2048, 2048], P('row', ('layer', 'col')), may hold values 0 or 1
Outputs:
- inflated: float32 [2048, 2048], P('row', ('layer', 'col'))
The draws below stay inside these ranges and needn't reach their ends.
Inputs may be any that keep to these rules, and one draw needn't show every extreme that they name: `a_pattern`: 1 marks a present tile, 0 an absent one. `c_pattern`: 1 marks a kept tile. `prune_mask`: 1 marks a surviving entry.
All inputs are finite; a program needn't handle non-finite values. No bound on the sum of `c_pattern` or of `prune_mask` on one device may be relied on, other than what follows from the above.
Results may differ from the reference program's by a relative error of at most 0.001.
Values may be sent and summed in bfloat16 or wider, within the bound.
No kernel may reach another device: no remote copies, remote signals or barrier semaphores. Data moves between devices by JAX's collectives and lax.ppermute only.
A program may use at most 64 MiB of HBM per device.

```python
import math
import jax
import jax.numpy as jnp
from jax import lax

TILE = 128
N = 2048
NT = 16


def draw_values(key, part):
    key = jax.random.fold_in(key, 11)
    first, second, third, fourth = jax.random.split(key, 4)
    position = jnp.arange(N, dtype=jnp.float32) / N
    base = jnp.exp(jnp.clip(jax.random.normal(first, (N, N), jnp.float32), -5.0, 5.0))
    keep = jax.random.uniform(fourth, (N, N), jnp.float32) < 0.7
    row_scale = jnp.exp(jax.random.uniform(second, (N,), jnp.float32, 0.0, math.log(3.2))) * jnp.sqrt(1.0 + 2.0 * position)
    col_scale = jnp.exp(jax.random.uniform(third, (N,), jnp.float32, 0.0, math.log(3.2)))
    scaled = base * keep.astype(jnp.float32) * row_scale[:, None] * col_scale[None, :] * (1.0 / (0.65 * N))
    return jnp.clip(scaled, 0.0, 2.0)


def draw_a_pattern(key, part):
    key = jax.random.fold_in(key, 23)
    first, second = jax.random.split(key)
    density = jax.random.randint(first, (NT, 1), 2, 9)
    ticket = jax.random.randint(second, (NT, NT), 0, 8)
    return (ticket < density).astype(jnp.int32)


def with_ends(entries, rng, smallest, top_value):
    longest = entries.shape.index(max(entries.shape))
    spots = []
    for shift in (0, 1):
        where = [jax.random.randint(jax.random.fold_in(rng, axis), (), 0, length) for axis, length in enumerate(entries.shape)]
        where[longest] = (where[longest] + shift) % entries.shape[longest]
        spots.append(tuple(where))
    return entries.at[spots[0]].set(smallest).at[spots[1]].set(top_value)


def setup_inputs(seed: int = 0) -> dict:
    key_list = jax.random.split(jax.random.key(seed), 5)
    values = draw_values(jax.random.fold_in(key_list[4], 71), 0)
    a_pattern = draw_a_pattern(jax.random.fold_in(key_list[4], 71), 0)
    c_pattern = with_ends((jax.random.randint(key_list[2], (NT, NT), 0, 4) < 3).astype(jnp.int32), jax.random.fold_in(key_list[2], 1), 0, 1)
    prune_mask = with_ends((jax.random.randint(key_list[3], (N, N), 0, 4) < 3).astype(jnp.int32), jax.random.fold_in(key_list[3], 1), 0, 1)
    return dict(values=values, a_pattern=a_pattern, c_pattern=c_pattern, prune_mask=prune_mask)


epsilon = 1e-9


def spread_tiles(pattern):
    tile_rows, tile_cols = pattern.shape
    blocked = jnp.broadcast_to(pattern.astype(jnp.float32)[:, None, :, None], (tile_rows, TILE, tile_cols, TILE))
    return blocked.reshape(tile_rows * TILE, tile_cols * TILE)


def reference(values, a_pattern, c_pattern, prune_mask):
    sparse = (values * spread_tiles(a_pattern)).astype(jnp.bfloat16)
    widened = sparse.astype(jnp.float32)
    product = jnp.dot(widened, widened, preferred_element_type=jnp.float32, precision=lax.Precision.HIGHEST)
    kept_tiles = product * spread_tiles(c_pattern)
    squares = kept_tiles * kept_tiles * prune_mask.astype(jnp.float32)
    column_sum = jnp.sum(squares, axis=0)
    return (N * squares) / (column_sum[None, :] + epsilon)
```

```python
import functools

import jax
import jax.numpy as jnp
from jax import lax
from jax.experimental import pallas as pl
from jax.experimental.pallas import tpu as pltpu
from jax.sharding import PartitionSpec as P

TILE = 128


epsilon = 1e-09

VMEM = pl.BlockSpec(memory_space=pltpu.VMEM)
SMEM = pl.BlockSpec(memory_space=pltpu.SMEM)


def spread_tiles(pattern):
    tile_rows, tile_cols = pattern.shape
    blocked = jnp.broadcast_to(
        pattern.astype(jnp.float32)[:, None, :, None], (tile_rows, TILE, tile_cols, TILE)
    )
    return blocked.reshape(tile_rows * TILE, tile_cols * TILE)


def tile_slices(shape):
    for i in range(shape[0] // TILE):
        for j in range(shape[1] // TILE):
            yield i, j, (slice(i * TILE, (i + 1) * TILE), slice(j * TILE, (j + 1) * TILE))


def sparse_kernel(values_ref, pattern_ref, out_ref):
    for i, j, at in tile_slices(values_ref.shape):
        present = pattern_ref[i, j].astype(jnp.float32)
        out_ref[at] = (values_ref[at] * present).astype(jnp.bfloat16)


def most_kernel(place_ref, *refs):
    left, right = refs[:6], refs[6:10]
    total_ref, own_ref, other_ref, panel_ref = refs[10:]
    lead, parity = place_ref[0], place_ref[1]
    half = left[0].shape[1]
    for s in range(4):
        panel_ref[s ^ lead] = right[s][...]
    total = None
    for s in range(3):
        for side in range(2):
            rows = pl.ds(pl.multiple_of((parity ^ side) * half, half), half)
            part = jnp.dot(left[2 * s + side][...], panel_ref[s, rows, :], preferred_element_type=jnp.float32)
            total = part if total is None else total + part
    total_ref[...] = total
    own_ref[...] = panel_ref[3, pl.ds(pl.multiple_of(parity * half, half), half), :]
    other_ref[...] = panel_ref[3, pl.ds(pl.multiple_of((1 - parity) * half, half), half), :]


def squares_kernel(pattern_ref, total_ref, left_own_ref, left_other_ref, own_ref, other_ref, mask_ref, squares_ref, sums_ref):
    product = total_ref[...] + jnp.dot(left_own_ref[...], own_ref[...], preferred_element_type=jnp.float32)
    product = product + jnp.dot(left_other_ref[...], other_ref[...], preferred_element_type=jnp.float32)
    columns = [None] * (product.shape[1] // TILE)
    for i, j, at in tile_slices(product.shape):
        kept = product[at] * pattern_ref[i, j].astype(jnp.float32)
        squares = kept * kept * mask_ref[at].astype(jnp.float32)
        squares_ref[at] = squares
        part = jnp.sum(squares.reshape(TILE // 8, 8, TILE), axis=0)
        columns[j] = part if columns[j] is None else columns[j] + part
    for j, part in enumerate(columns):
        sums_ref[:, j * TILE:(j + 1) * TILE] = part


def scale_kernel(total_rows, squares_ref, *refs):
    sums, out_ref = refs[:-1], refs[-1]
    column = sums[0][...]
    for other in sums[1:]:
        column = column + other[...]
    column = jnp.sum(column, axis=0, keepdims=True) + epsilon
    out_ref[...] = total_rows * squares_ref[...] / column


def swap(x, axis, size, s):
    return lax.ppermute(x, axis, [(i, i ^ s) for i in range(size)])


def after(x, *others):
    return lax.optimization_barrier((x,) + others)[0]


def call(kernel, out_shape, in_specs, flops=0, size=0, **options):
    return pl.pallas_call(
        kernel,
        out_shape=out_shape,
        in_specs=in_specs,
        out_specs=jax.tree.map(lambda _: VMEM, out_shape),
        compiler_params=pltpu.CompilerParams(vmem_limit_bytes=16 * 2**20),
        cost_estimate=pl.CostEstimate(flops=flops, bytes_accessed=size, transcendentals=0),
        **options,
    )


def on_small_mesh(values, a_pattern, c_pattern, prune_mask):
    rows, cols = values.shape
    row, col, layer = lax.axis_index("row"), lax.axis_index("col"), lax.axis_index("layer")
    total_rows = rows * 4
    block = jax.ShapeDtypeStruct((rows, cols), jnp.bfloat16)
    full = jax.ShapeDtypeStruct((rows, cols), jnp.float32)

    own = call(sparse_kernel, block, [VMEM, SMEM], size=6 * rows * cols)(values, a_pattern)
    near2 = swap(own, "layer", 4, 2)
    near1 = swap(own, "layer", 4, 1)
    right = [own] + [swap(own, "row", 4, s) for s in (1, 2, 3)]
    own_late = after(own, near2)
    ends = lax.ppermute(near2, "layer", [(2, 3), (1, 0)])
    middle = lax.ppermute(own_late, "layer", [(1, 2), (2, 1)])
    left = []
    for x in (own, near1, near2):
        left += [x, swap(x, "col", 2, 1)]
    place = jnp.stack([row ^ layer, col]).astype(jnp.int32)
    total, last_own, last_other = call(
        most_kernel,
        [full, jax.ShapeDtypeStruct((cols, cols), jnp.bfloat16), jax.ShapeDtypeStruct((cols, cols), jnp.bfloat16)],
        [SMEM] + [VMEM] * 10,
        flops=2 * rows * cols * 3 * rows,
        size=2 * 10 * rows * cols,
        scratch_shapes=[pltpu.VMEM((4, rows, cols), jnp.bfloat16)],
    )(place, *left, *right)
    far = ends + middle
    far_other = swap(far, "col", 2, 1)
    squares, sums = call(
        squares_kernel,
        [full, jax.ShapeDtypeStruct((8, cols), jnp.float32)],
        [SMEM] + [VMEM] * 6,
        flops=2 * rows * cols * rows,
        size=16 * rows * cols,
    )(c_pattern, total, far, far_other, last_own, last_other, prune_mask)
    others = [swap(sums, "row", 4, s) for s in (1, 2, 3)]
    return call(
        functools.partial(scale_kernel, total_rows), full, [VMEM] * 5, flops=4 * rows * cols, size=8 * rows * cols
    )(squares, sums, *others)


def on_any_mesh(values, a_pattern, c_pattern, prune_mask):
    total_rows = values.shape[0] * lax.axis_size("row")
    sparse = (values * spread_tiles(a_pattern)).astype(jnp.bfloat16)
    left = lax.all_gather(sparse, ("layer", "col"), axis=1, tiled=True)
    right = lax.all_gather(sparse, "row", axis=0, tiled=True)
    kept = jnp.dot(left, right, preferred_element_type=jnp.float32) * spread_tiles(c_pattern)
    squares = kept * kept * prune_mask.astype(jnp.float32)
    column_sums = lax.psum(jnp.sum(squares, axis=0), "row")
    return total_rows * squares / (column_sums[None, :] + epsilon)


def solution(mesh):
    spec = P("row", ("layer", "col"))
    sizes = tuple(mesh.shape[name] for name in ("row", "col", "layer"))
    on_device = on_small_mesh if sizes == (4, 2, 4) else on_any_mesh
    return jax.shard_map(on_device, mesh=mesh, in_specs=(spec,) * 4, out_specs=spec, check_vma=False)
```

```python
import functools

import jax
import jax.numpy as jnp
from jax import lax
from jax.experimental import pallas as pl
from jax.experimental.pallas import tpu as pltpu
from jax.sharding import PartitionSpec as P

TILE = 128


epsilon = 1e-09

VMEM = pl.BlockSpec(memory_space=pltpu.VMEM)


def spread_tiles(pattern):
    tile_rows, tile_cols = pattern.shape
    blocked = jnp.broadcast_to(
        pattern.astype(jnp.float32)[:, None, :, None], (tile_rows, TILE, tile_cols, TILE)
    )
    return blocked.reshape(tile_rows * TILE, tile_cols * TILE)


def times_tiles(x, pattern):
    tile_rows, tile_cols = pattern.shape
    tiles = x.reshape(tile_rows, TILE, tile_cols, TILE) * pattern[:, None, :, None]
    return tiles.reshape(x.shape)


def most_kernel(*refs):
    here, there, right = refs[:3], refs[3:6], refs[6:10]
    total_ref, own_ref, other_ref, panel_ref = refs[10:]
    parity = lax.axis_index("col")
    lead = lax.axis_index("row") ^ lax.axis_index("layer")
    half = here[0].shape[1]
    for s in range(4):
        panel_ref[s ^ lead] = right[s][...]
    total = None
    for s in range(3):
        for side, block in enumerate((here[s], there[s])):
            rows = pl.ds(pl.multiple_of((parity ^ side) * half, half), half)
            part = jnp.dot(block[...], panel_ref[s, rows, :], preferred_element_type=jnp.float32)
            total = part if total is None else total + part
    total_ref[...] = total
    own_ref[...] = panel_ref[3, pl.ds(pl.multiple_of(parity * half, half), half), :]
    other_ref[...] = panel_ref[3, pl.ds(pl.multiple_of((1 - parity) * half, half), half), :]


def squares_kernel(total_ref, left_own_ref, left_other_ref, own_ref, other_ref, weight_ref, squares_ref, sums_ref):
    product = total_ref[...] + jnp.dot(left_own_ref[...], own_ref[...], preferred_element_type=jnp.float32)
    product = product + jnp.dot(left_other_ref[...], other_ref[...], preferred_element_type=jnp.float32)
    squares = product * product * weight_ref[...]
    squares_ref[...] = squares
    rows, cols = squares.shape
    sums_ref[...] = jnp.sum(squares.reshape(rows // 8, 8, cols), axis=0)


def scale_kernel(total_rows, squares_ref, *refs):
    sums, out_ref = refs[:-1], refs[-1]
    column = sums[0][...]
    for other in sums[1:]:
        column = column + other[...]
    column = jnp.sum(column, axis=0, keepdims=True) + epsilon
    out_ref[...] = total_rows * squares_ref[...] / column


def swap(x, axis, size, s):
    return lax.ppermute(x, axis, [(i, i ^ s) for i in range(size)])


def call(kernel, out_shape, in_specs, flops=0, size=0, **options):
    return pl.pallas_call(
        kernel,
        out_shape=out_shape,
        in_specs=in_specs,
        out_specs=jax.tree.map(lambda _: VMEM, out_shape),
        compiler_params=pltpu.CompilerParams(vmem_limit_bytes=16 * 2**20),
        cost_estimate=pl.CostEstimate(flops=flops, bytes_accessed=size, transcendentals=0),
        **options,
    )


def on_small_mesh(values, a_pattern, c_pattern, prune_mask):
    rows, cols = values.shape
    total_rows = rows * 4
    full = jax.ShapeDtypeStruct((rows, cols), jnp.float32)

    own = times_tiles(values, a_pattern.astype(jnp.float32)).astype(jnp.bfloat16)
    near2 = swap(own, "layer", 4, 2)
    near1 = swap(own, "layer", 4, 1)
    right = [own] + [swap(own, "row", 4, s) for s in (1, 2, 3)]
    weight = times_tiles(prune_mask.astype(jnp.float32), c_pattern.astype(jnp.float32))
    near2, *right, near1, weight = lax.optimization_barrier((near2, *right, near1, weight))
    ends = lax.ppermute(near2, "layer", [(2, 3), (1, 0)])
    far = lax.ppermute(right[0], "layer", [(1, 2), (2, 1)])
    here = [own, near1, near2]
    there = [swap(x, "col", 2, 1) for x in here]
    ends, far = lax.optimization_barrier((ends, far))
    far = ends + far
    far_other = swap(far, "col", 2, 1)
    total, last_own, last_other = call(
        most_kernel,
        [full, jax.ShapeDtypeStruct((cols, cols), jnp.bfloat16), jax.ShapeDtypeStruct((cols, cols), jnp.bfloat16)],
        [VMEM] * 10,
        flops=2 * rows * cols * 3 * rows,
        size=2 * 10 * rows * cols,
        scratch_shapes=[pltpu.VMEM((4, rows, cols), jnp.bfloat16)],
    )(*here, *there, *right)
    squares, sums = call(
        squares_kernel,
        [full, jax.ShapeDtypeStruct((8, cols), jnp.float32)],
        [VMEM] * 6,
        flops=2 * rows * cols * rows,
        size=16 * rows * cols,
    )(total, far, far_other, last_own, last_other, weight)
    others = [swap(sums, "row", 4, s) for s in (1, 2, 3)]
    return call(
        functools.partial(scale_kernel, total_rows), full, [VMEM] * 5, flops=4 * rows * cols, size=8 * rows * cols
    )(squares, sums, *others)


def on_any_mesh(values, a_pattern, c_pattern, prune_mask):
    total_rows = values.shape[0] * lax.axis_size("row")
    sparse = (values * spread_tiles(a_pattern)).astype(jnp.bfloat16)
    left = lax.all_gather(sparse, ("layer", "col"), axis=1, tiled=True)
    right = lax.all_gather(sparse, "row", axis=0, tiled=True)
    kept = jnp.dot(left, right, preferred_element_type=jnp.float32) * spread_tiles(c_pattern)
    squares = kept * kept * prune_mask.astype(jnp.float32)
    column_sums = lax.psum(jnp.sum(squares, axis=0), "row")
    return total_rows * squares / (column_sums[None, :] + epsilon)


def solution(mesh):
    spec = P("row", ("layer", "col"))
    sizes = tuple(mesh.shape[name] for name in ("row", "col", "layer"))
    on_device = on_small_mesh if sizes == (4, 2, 4) else on_any_mesh
    return jax.shard_map(on_device, mesh=mesh, in_specs=(spec,) * 4, out_specs=spec, check_vma=False)
```

```python
import functools

import jax
import jax.numpy as jnp
from jax import lax
from jax.experimental import pallas as pl
from jax.experimental.pallas import tpu as pltpu
from jax.sharding import PartitionSpec as P

TILE = 128


epsilon = 1e-09

VMEM = pl.BlockSpec(memory_space=pltpu.VMEM)


def spread_tiles(pattern):
    tile_rows, tile_cols = pattern.shape
    blocked = jnp.broadcast_to(
        pattern.astype(jnp.float32)[:, None, :, None], (tile_rows, TILE, tile_cols, TILE)
    )
    return blocked.reshape(tile_rows * TILE, tile_cols * TILE)


def times_tiles(x, pattern):
    tile_rows, tile_cols = pattern.shape
    tiles = x.reshape(tile_rows, TILE, tile_cols, TILE) * pattern[:, None, :, None]
    return tiles.reshape(x.shape)


def most_kernel(*refs):
    right, here, there = refs[:4], refs[4:7], refs[7:10]
    total_ref, own_ref, other_ref, panel_ref = refs[10:]
    parity = lax.axis_index("col")
    lead = lax.axis_index("row") ^ lax.axis_index("layer")
    half = here[0].shape[1]
    for s in range(4):
        panel_ref[s ^ lead] = right[s][...]
    total = None
    for s in range(3):
        for side, block in enumerate((here[s], there[s])):
            rows = pl.ds(pl.multiple_of((parity ^ side) * half, half), half)
            part = jnp.dot(block[...], panel_ref[s, rows, :], preferred_element_type=jnp.float32)
            total = part if total is None else total + part
    total_ref[...] = total
    own_ref[...] = panel_ref[3, pl.ds(pl.multiple_of(parity * half, half), half), :]
    other_ref[...] = panel_ref[3, pl.ds(pl.multiple_of((1 - parity) * half, half), half), :]


def squares_kernel(total_ref, left_own_ref, left_other_ref, own_ref, other_ref, weight_ref, squares_ref, sums_ref):
    product = total_ref[...] + jnp.dot(left_own_ref[...], own_ref[...], preferred_element_type=jnp.float32)
    product = product + jnp.dot(left_other_ref[...], other_ref[...], preferred_element_type=jnp.float32)
    squares = product * product * weight_ref[...]
    squares_ref[...] = squares
    rows, cols = squares.shape
    sums_ref[...] = jnp.sum(squares.reshape(rows // 8, 8, cols), axis=0)


def scale_kernel(total_rows, squares_ref, *refs):
    sums, out_ref = refs[:-1], refs[-1]
    column = sums[0][...]
    for other in sums[1:]:
        column = column + other[...]
    column = jnp.sum(column, axis=0, keepdims=True) + epsilon
    out_ref[...] = total_rows * squares_ref[...] / column


def swap(x, axis, size, s):
    return lax.ppermute(x, axis, [(i, i ^ s) for i in range(size)])


def call(kernel, out_shape, in_specs, flops=0, size=0, **options):
    return pl.pallas_call(
        kernel,
        out_shape=out_shape,
        in_specs=in_specs,
        out_specs=jax.tree.map(lambda _: VMEM, out_shape),
        compiler_params=pltpu.CompilerParams(vmem_limit_bytes=16 * 2**20),
        cost_estimate=pl.CostEstimate(flops=flops, bytes_accessed=size, transcendentals=0),
        **options,
    )


def on_small_mesh(values, a_pattern, c_pattern, prune_mask):
    rows, cols = values.shape
    total_rows = rows * 4
    full = jax.ShapeDtypeStruct((rows, cols), jnp.float32)

    own = times_tiles(values, a_pattern.astype(jnp.float32)).astype(jnp.bfloat16)
    near2 = swap(own, "layer", 4, 2)
    near1 = swap(own, "layer", 4, 1)
    right = [own] + [swap(own, "row", 4, s) for s in (1, 2)]
    weight = times_tiles(prune_mask.astype(jnp.float32), c_pattern.astype(jnp.float32))
    own_there = swap(own, "col", 2, 1)
    near2, near1, right[1], right[2], own_there, start, weight = lax.optimization_barrier(
        (near2, near1, right[1], right[2], own_there, own, weight)
    )
    ends = lax.ppermute(near2, "layer", [(2, 3), (1, 0)])
    far = lax.ppermute(start, "layer", [(1, 2), (2, 1)])
    right.append(swap(start, "row", 4, 3))
    here = [own, near1, near2]
    there = [own_there] + [swap(x, "col", 2, 1) for x in here[1:]]
    ends, far = lax.optimization_barrier((ends, far))
    far = ends + far
    far_other = swap(far, "col", 2, 1)
    total, last_own, last_other = call(
        most_kernel,
        [full, jax.ShapeDtypeStruct((cols, cols), jnp.bfloat16), jax.ShapeDtypeStruct((cols, cols), jnp.bfloat16)],
        [VMEM] * 10,
        flops=2 * rows * cols * 3 * rows,
        size=2 * 10 * rows * cols,
        scratch_shapes=[pltpu.VMEM((4, rows, cols), jnp.bfloat16)],
    )(*right, *here, *there)
    squares, sums = call(
        squares_kernel,
        [full, jax.ShapeDtypeStruct((8, cols), jnp.float32)],
        [VMEM] * 6,
        flops=2 * rows * cols * rows,
        size=16 * rows * cols,
    )(total, far, far_other, last_own, last_other, weight)
    others = [swap(sums, "row", 4, s) for s in (1, 2, 3)]
    return call(
        functools.partial(scale_kernel, total_rows), full, [VMEM] * 5, flops=4 * rows * cols, size=8 * rows * cols
    )(squares, sums, *others)


def on_any_mesh(values, a_pattern, c_pattern, prune_mask):
    total_rows = values.shape[0] * lax.axis_size("row")
    sparse = (values * spread_tiles(a_pattern)).astype(jnp.bfloat16)
    left = lax.all_gather(sparse, ("layer", "col"), axis=1, tiled=True)
    right = lax.all_gather(sparse, "row", axis=0, tiled=True)
    kept = jnp.dot(left, right, preferred_element_type=jnp.float32) * spread_tiles(c_pattern)
    squares = kept * kept * prune_mask.astype(jnp.float32)
    column_sums = lax.psum(jnp.sum(squares, axis=0), "row")
    return total_rows * squares / (column_sums[None, :] + epsilon)


def solution(mesh):
    spec = P("row", ("layer", "col"))
    sizes = tuple(mesh.shape[name] for name in ("row", "col", "layer"))
    on_device = on_small_mesh if sizes == (4, 2, 4) else on_any_mesh
    return jax.shard_map(on_device, mesh=mesh, in_specs=(spec,) * 4, out_specs=spec, check_vma=False)
```

```python
import functools

import jax
import jax.numpy as jnp
from jax import lax
from jax.experimental import pallas as pl
from jax.experimental.pallas import tpu as pltpu
from jax.sharding import PartitionSpec as P

TILE = 128


epsilon = 1e-09

VMEM = pl.BlockSpec(memory_space=pltpu.VMEM)


def spread_tiles(pattern):
    tile_rows, tile_cols = pattern.shape
    blocked = jnp.broadcast_to(
        pattern.astype(jnp.float32)[:, None, :, None], (tile_rows, TILE, tile_cols, TILE)
    )
    return blocked.reshape(tile_rows * TILE, tile_cols * TILE)


def times_tiles(x, pattern):
    tile_rows, tile_cols = pattern.shape
    tiles = x.reshape(tile_rows, TILE, tile_cols, TILE) * pattern[:, None, :, None]
    return tiles.reshape(x.shape)


def most_kernel(*refs):
    right, here, there = refs[:4], refs[4:7], refs[7:10]
    total_ref, own_ref, other_ref, panel_ref = refs[10:]
    parity = lax.axis_index("col")
    layer = lax.axis_index("layer")
    lead = lax.axis_index("row") ^ layer
    middle = (layer ^ (layer >> 1)) & 1
    half = here[0].shape[1]
    for s in range(4):
        panel_ref[s ^ lead] = right[s][...]
    total = None
    for s, distance in enumerate((0, 1 + middle, 2 - middle)):
        for side, block in enumerate((here[s], there[s])):
            rows = pl.ds(pl.multiple_of((parity ^ side) * half, half), half)
            part = jnp.dot(block[...], panel_ref[distance, rows, :], preferred_element_type=jnp.float32)
            total = part if total is None else total + part
    total_ref[...] = total
    own_ref[...] = panel_ref[3, pl.ds(pl.multiple_of(parity * half, half), half), :]
    other_ref[...] = panel_ref[3, pl.ds(pl.multiple_of((1 - parity) * half, half), half), :]


def squares_kernel(total_ref, left_own_ref, left_other_ref, own_ref, other_ref, weight_ref, squares_ref, sums_ref):
    product = total_ref[...] + jnp.dot(left_own_ref[...], own_ref[...], preferred_element_type=jnp.float32)
    product = product + jnp.dot(left_other_ref[...], other_ref[...], preferred_element_type=jnp.float32)
    squares = product * product * weight_ref[...]
    squares_ref[...] = squares
    rows, cols = squares.shape
    sums_ref[...] = jnp.sum(squares.reshape(rows // 8, 8, cols), axis=0)


def scale_kernel(total_rows, squares_ref, *refs):
    sums, out_ref = refs[:-1], refs[-1]
    column = sums[0][...]
    for other in sums[1:]:
        column = column + other[...]
    column = jnp.sum(column, axis=0, keepdims=True) + epsilon
    out_ref[...] = total_rows * squares_ref[...] / column


def swap(x, axis, size, s):
    return lax.ppermute(x, axis, [(i, i ^ s) for i in range(size)])


def call(kernel, out_shape, in_specs, flops=0, size=0, **options):
    return pl.pallas_call(
        kernel,
        out_shape=out_shape,
        in_specs=in_specs,
        out_specs=jax.tree.map(lambda _: VMEM, out_shape),
        compiler_params=pltpu.CompilerParams(vmem_limit_bytes=16 * 2**20),
        cost_estimate=pl.CostEstimate(flops=flops, bytes_accessed=size, transcendentals=0),
        **options,
    )


def on_small_mesh(values, a_pattern, c_pattern, prune_mask):
    rows, cols = values.shape
    total_rows = rows * 4
    full = jax.ShapeDtypeStruct((rows, cols), jnp.float32)

    own = times_tiles(values, a_pattern.astype(jnp.float32)).astype(jnp.bfloat16)
    first = lax.ppermute(own, "layer", [(0, 2), (3, 1), (1, 0), (2, 3)])
    second = lax.ppermute(own, "layer", [(0, 1), (3, 2), (1, 3), (2, 0)])
    right = [own] + [swap(own, "row", 4, s) for s in (1, 2, 3)]
    weight = times_tiles(prune_mask.astype(jnp.float32), c_pattern.astype(jnp.float32))
    first, start, weight = lax.optimization_barrier((first, own, weight))
    far = lax.ppermute(start, "layer", [(1, 2), (2, 1)])
    ends = lax.ppermute(first, "layer", [(1, 0), (2, 3)])
    second, right[3], right[2], right[1], first, start = lax.optimization_barrier((second, right[3], right[2], right[1], first, start))
    here = [start, first, second]
    there = [swap(x, "col", 2, 1) for x in here]
    far, ends, *there = lax.optimization_barrier((far, ends, *there))
    far = ends + far
    far_other = swap(far, "col", 2, 1)
    total, last_own, last_other = call(
        most_kernel,
        [full, jax.ShapeDtypeStruct((cols, cols), jnp.bfloat16), jax.ShapeDtypeStruct((cols, cols), jnp.bfloat16)],
        [VMEM] * 10,
        flops=2 * rows * cols * 3 * rows,
        size=2 * 10 * rows * cols,
        scratch_shapes=[pltpu.VMEM((4, rows, cols), jnp.bfloat16)],
    )(*right, *here, *there)
    squares, sums = call(
        squares_kernel,
        [full, jax.ShapeDtypeStruct((8, cols), jnp.float32)],
        [VMEM] * 6,
        flops=2 * rows * cols * rows,
        size=16 * rows * cols,
    )(total, far, far_other, last_own, last_other, weight)
    others = [swap(sums, "row", 4, s) for s in (1, 2, 3)]
    return call(
        functools.partial(scale_kernel, total_rows), full, [VMEM] * 5, flops=4 * rows * cols, size=8 * rows * cols
    )(squares, sums, *others)


def on_any_mesh(values, a_pattern, c_pattern, prune_mask):
    total_rows = values.shape[0] * lax.axis_size("row")
    sparse = (values * spread_tiles(a_pattern)).astype(jnp.bfloat16)
    left = lax.all_gather(sparse, ("layer", "col"), axis=1, tiled=True)
    right = lax.all_gather(sparse, "row", axis=0, tiled=True)
    kept = jnp.dot(left, right, preferred_element_type=jnp.float32) * spread_tiles(c_pattern)
    squares = kept * kept * prune_mask.astype(jnp.float32)
    column_sums = lax.psum(jnp.sum(squares, axis=0), "row")
    return total_rows * squares / (column_sums[None, :] + epsilon)


def solution(mesh):
    spec = P("row", ("layer", "col"))
    sizes = tuple(mesh.shape[name] for name in ("row", "col", "layer"))
    on_device = on_small_mesh if sizes == (4, 2, 4) else on_any_mesh
    return jax.shard_map(on_device, mesh=mesh, in_specs=(spec,) * 4, out_specs=spec, check_vma=False)
```

```python
import functools

import jax
import jax.numpy as jnp
from jax import lax
from jax.experimental import pallas as pl
from jax.experimental.pallas import tpu as pltpu
from jax.sharding import PartitionSpec as P

TILE = 128


epsilon = 1e-09

VMEM = pl.BlockSpec(memory_space=pltpu.VMEM)


def spread_tiles(pattern):
    tile_rows, tile_cols = pattern.shape
    blocked = jnp.broadcast_to(
        pattern.astype(jnp.float32)[:, None, :, None], (tile_rows, TILE, tile_cols, TILE)
    )
    return blocked.reshape(tile_rows * TILE, tile_cols * TILE)


def times_tiles(x, pattern):
    tile_rows, tile_cols = pattern.shape
    tiles = x.reshape(tile_rows, TILE, tile_cols, TILE) * pattern[:, None, :, None]
    return tiles.reshape(x.shape)


def most_kernel(*refs):
    right, here, there = refs[:4], refs[4:7], refs[7:10]
    total_ref, own_ref, other_ref, panel_ref = refs[10:]
    parity = lax.axis_index("col")
    layer = lax.axis_index("layer")
    lead = lax.axis_index("row") ^ layer
    middle = (layer ^ (layer >> 1)) & 1
    half = here[0].shape[1]
    for s in range(4):
        panel_ref[s ^ lead] = right[s][...]
    total = None
    for s, distance in enumerate((0, 1 + middle, 2 - middle)):
        for side, block in enumerate((here[s], there[s])):
            rows = pl.ds(pl.multiple_of((parity ^ side) * half, half), half)
            part = jnp.dot(block[...], panel_ref[distance, rows, :], preferred_element_type=jnp.float32)
            total = part if total is None else total + part
    total_ref[...] = total
    own_ref[...] = panel_ref[3, pl.ds(pl.multiple_of(parity * half, half), half), :]
    other_ref[...] = panel_ref[3, pl.ds(pl.multiple_of((1 - parity) * half, half), half), :]


def squares_kernel(total_ref, left_own_ref, left_other_ref, own_ref, other_ref, weight_ref, squares_ref, sums_ref):
    product = total_ref[...] + jnp.dot(left_own_ref[...], own_ref[...], preferred_element_type=jnp.float32)
    product = product + jnp.dot(left_other_ref[...], other_ref[...], preferred_element_type=jnp.float32)
    squares = product * product * weight_ref[...]
    squares_ref[...] = squares
    rows, cols = squares.shape
    sums_ref[...] = jnp.sum(squares.reshape(rows // 8, 8, cols), axis=0)


def scale_kernel(total_rows, squares_ref, *refs):
    sums, out_ref = refs[:-1], refs[-1]
    column = sums[0][...]
    for other in sums[1:]:
        column = column + other[...]
    column = jnp.sum(column, axis=0, keepdims=True) + epsilon
    out_ref[...] = total_rows * squares_ref[...] / column


def swap(x, axis, size, s):
    return lax.ppermute(x, axis, [(i, i ^ s) for i in range(size)])


def call(kernel, out_shape, in_specs, flops=0, size=0, **options):
    return pl.pallas_call(
        kernel,
        out_shape=out_shape,
        in_specs=in_specs,
        out_specs=jax.tree.map(lambda _: VMEM, out_shape),
        compiler_params=pltpu.CompilerParams(vmem_limit_bytes=16 * 2**20),
        cost_estimate=pl.CostEstimate(flops=flops, bytes_accessed=size, transcendentals=0),
        **options,
    )


def on_small_mesh(values, a_pattern, c_pattern, prune_mask):
    rows, cols = values.shape
    total_rows = rows * 4
    full = jax.ShapeDtypeStruct((rows, cols), jnp.float32)

    own = times_tiles(values, a_pattern.astype(jnp.float32)).astype(jnp.bfloat16)
    ring = [(0, 2), (2, 3), (3, 1), (1, 0)]
    first = lax.ppermute(own, "layer", ring)
    second = lax.ppermute(own, "layer", [(b, a) for a, b in ring])
    right = [own] + [swap(own, "row", 4, s) for s in (1, 2, 3)]
    weight = times_tiles(prune_mask.astype(jnp.float32), c_pattern.astype(jnp.float32))
    first, start, weight = lax.optimization_barrier((first, own, weight))
    far = lax.ppermute(first, "layer", ring)
    second, right[3], right[2], right[1], first, start = lax.optimization_barrier((second, right[3], right[2], right[1], first, start))
    here = [start, first, second]
    there = [swap(x, "col", 2, 1) for x in here]
    far, *there = lax.optimization_barrier((far, *there))
    far_other = swap(far, "col", 2, 1)
    total, last_own, last_other = call(
        most_kernel,
        [full, jax.ShapeDtypeStruct((cols, cols), jnp.bfloat16), jax.ShapeDtypeStruct((cols, cols), jnp.bfloat16)],
        [VMEM] * 10,
        flops=2 * rows * cols * 3 * rows,
        size=2 * 10 * rows * cols,
        scratch_shapes=[pltpu.VMEM((4, rows, cols), jnp.bfloat16)],
    )(*right, *here, *there)
    squares, sums = call(
        squares_kernel,
        [full, jax.ShapeDtypeStruct((8, cols), jnp.float32)],
        [VMEM] * 6,
        flops=2 * rows * cols * rows,
        size=16 * rows * cols,
    )(total, far, far_other, last_own, last_other, weight)
    others = [swap(sums, "row", 4, s) for s in (1, 2, 3)]
    return call(
        functools.partial(scale_kernel, total_rows), full, [VMEM] * 5, flops=4 * rows * cols, size=8 * rows * cols
    )(squares, sums, *others)


def on_any_mesh(values, a_pattern, c_pattern, prune_mask):
    total_rows = values.shape[0] * lax.axis_size("row")
    sparse = (values * spread_tiles(a_pattern)).astype(jnp.bfloat16)
    left = lax.all_gather(sparse, ("layer", "col"), axis=1, tiled=True)
    right = lax.all_gather(sparse, "row", axis=0, tiled=True)
    kept = jnp.dot(left, right, preferred_element_type=jnp.float32) * spread_tiles(c_pattern)
    squares = kept * kept * prune_mask.astype(jnp.float32)
    column_sums = lax.psum(jnp.sum(squares, axis=0), "row")
    return total_rows * squares / (column_sums[None, :] + epsilon)


def solution(mesh):
    spec = P("row", ("layer", "col"))
    sizes = tuple(mesh.shape[name] for name in ("row", "col", "layer"))
    on_device = on_small_mesh if sizes == (4, 2, 4) else on_any_mesh
    return jax.shard_map(on_device, mesh=mesh, in_specs=(spec,) * 4, out_specs=spec, check_vma=False)
```

```python
import functools

import jax
import jax.numpy as jnp
from jax import lax
from jax.experimental import pallas as pl
from jax.experimental.pallas import tpu as pltpu
from jax.sharding import PartitionSpec as P

TILE = 128


epsilon = 1e-09

VMEM = pl.BlockSpec(memory_space=pltpu.VMEM)


def spread_tiles(pattern):
    tile_rows, tile_cols = pattern.shape
    blocked = jnp.broadcast_to(
        pattern.astype(jnp.float32)[:, None, :, None], (tile_rows, TILE, tile_cols, TILE)
    )
    return blocked.reshape(tile_rows * TILE, tile_cols * TILE)


def times_tiles(x, pattern):
    tile_rows, tile_cols = pattern.shape
    tiles = x.reshape(tile_rows, TILE, tile_cols, TILE) * pattern[:, None, :, None]
    return tiles.reshape(x.shape)


def most_kernel(*refs):
    right, here, there = refs[:4], refs[4:8], list(refs[8:11])
    total_ref, other_ref, panel_ref = refs[11:]
    parity = lax.axis_index("col")
    layer = lax.axis_index("layer")
    lead = lax.axis_index("row") ^ layer
    middle = (layer ^ (layer >> 1)) & 1
    half = here[0].shape[1]
    for s in range(4):
        panel_ref[s ^ lead] = right[s][...]
    total = None
    for s, distance in enumerate((0, 1 + middle, 2 - middle, 3)):
        for side, block in enumerate([here[s]] + there[s : s + 1]):
            rows = pl.ds(pl.multiple_of((parity ^ side) * half, half), half)
            part = jnp.dot(block[...], panel_ref[distance, rows, :], preferred_element_type=jnp.float32)
            total = part if total is None else total + part
    total_ref[...] = total
    other_ref[...] = panel_ref[3, pl.ds(pl.multiple_of((1 - parity) * half, half), half), :]


def squares_kernel(total_ref, left_ref, right_ref, weight_ref, squares_ref, sums_ref):
    product = total_ref[...] + jnp.dot(left_ref[...], right_ref[...], preferred_element_type=jnp.float32)
    squares = product * product * weight_ref[...]
    squares_ref[...] = squares
    rows, cols = squares.shape
    sums_ref[...] = jnp.sum(squares, axis=0, keepdims=True)


def scale_kernel(total_rows, squares_ref, *refs):
    sums, out_ref = refs[:-1], refs[-1]
    column = sums[0][...]
    for other in sums[1:]:
        column = column + other[...]
    column = column + epsilon
    out_ref[...] = total_rows * squares_ref[...] / column


def swap(x, axis, size, s):
    return lax.ppermute(x, axis, [(i, i ^ s) for i in range(size)])


def call(kernel, out_shape, in_specs, flops=0, size=0, **options):
    return pl.pallas_call(
        kernel,
        out_shape=out_shape,
        in_specs=in_specs,
        out_specs=jax.tree.map(lambda _: VMEM, out_shape),
        compiler_params=pltpu.CompilerParams(vmem_limit_bytes=16 * 2**20),
        cost_estimate=pl.CostEstimate(flops=flops, bytes_accessed=size, transcendentals=0),
        **options,
    )


def on_small_mesh(values, a_pattern, c_pattern, prune_mask):
    rows, cols = values.shape
    total_rows = rows * 4
    full = jax.ShapeDtypeStruct((rows, cols), jnp.float32)

    own = times_tiles(values, a_pattern.astype(jnp.float32)).astype(jnp.bfloat16)
    ring = [(0, 2), (2, 3), (3, 1), (1, 0)]
    first = lax.ppermute(own, "layer", ring)
    second = lax.ppermute(own, "layer", [(b, a) for a, b in ring])
    right = [own] + [swap(own, "row", 4, s) for s in (1, 2, 3)]
    weight = times_tiles(prune_mask.astype(jnp.float32), c_pattern.astype(jnp.float32))
    first, start, weight = lax.optimization_barrier((first, own, weight))
    far = lax.ppermute(first, "layer", ring)
    second, right[3], right[2], right[1], first, start = lax.optimization_barrier((second, right[3], right[2], right[1], first, start))
    here = [start, first, second]
    there = [swap(x, "col", 2, 1) for x in here]
    far, *there = lax.optimization_barrier((far, *there))
    far_other = swap(far, "col", 2, 1)
    total, last = call(
        most_kernel,
        [full, jax.ShapeDtypeStruct((cols, cols), jnp.bfloat16)],
        [VMEM] * 11,
        flops=2 * rows * cols * 3 * rows,
        size=2 * 10 * rows * cols,
        scratch_shapes=[pltpu.VMEM((4, rows, cols), jnp.bfloat16)],
    )(*right, *here, far, *there)
    squares, sums = call(
        squares_kernel,
        [full, jax.ShapeDtypeStruct((1, cols), jnp.float32)],
        [VMEM] * 4,
        flops=2 * rows * cols * rows,
        size=16 * rows * cols,
    )(total, far_other, last, weight)
    others = [swap(sums, "row", 4, s) for s in (1, 2, 3)]
    return call(
        functools.partial(scale_kernel, total_rows), full, [VMEM] * 5, flops=4 * rows * cols, size=8 * rows * cols
    )(squares, sums, *others)


def on_any_mesh(values, a_pattern, c_pattern, prune_mask):
    total_rows = values.shape[0] * lax.axis_size("row")
    sparse = (values * spread_tiles(a_pattern)).astype(jnp.bfloat16)
    left = lax.all_gather(sparse, ("layer", "col"), axis=1, tiled=True)
    right = lax.all_gather(sparse, "row", axis=0, tiled=True)
    kept = jnp.dot(left, right, preferred_element_type=jnp.float32) * spread_tiles(c_pattern)
    squares = kept * kept * prune_mask.astype(jnp.float32)
    column_sums = lax.psum(jnp.sum(squares, axis=0), "row")
    return total_rows * squares / (column_sums[None, :] + epsilon)


def solution(mesh):
    spec = P("row", ("layer", "col"))
    sizes = tuple(mesh.shape[name] for name in ("row", "col", "layer"))
    on_device = on_small_mesh if sizes == (4, 2, 4) else on_any_mesh
    return jax.shard_map(on_device, mesh=mesh, in_specs=(spec,) * 4, out_specs=spec, check_vma=False)
```

```python
import functools

import jax
import jax.numpy as jnp
from jax import lax
from jax.experimental import pallas as pl
from jax.experimental.pallas import tpu as pltpu
from jax.sharding import PartitionSpec as P

TILE = 128


epsilon = 1e-09

VMEM = pl.BlockSpec(memory_space=pltpu.VMEM)


def spread_tiles(pattern):
    tile_rows, tile_cols = pattern.shape
    blocked = jnp.broadcast_to(
        pattern.astype(jnp.float32)[:, None, :, None], (tile_rows, TILE, tile_cols, TILE)
    )
    return blocked.reshape(tile_rows * TILE, tile_cols * TILE)


def times_tiles(x, pattern):
    tile_rows, tile_cols = pattern.shape
    tiles = x.reshape(tile_rows, TILE, tile_cols, TILE) * pattern[:, None, :, None]
    return tiles.reshape(x.shape)


def most_kernel(*refs):
    right, here, there = refs[:4], refs[4:8], list(refs[8:11])
    total_ref, other_ref, panel_ref = refs[11:]
    parity = lax.axis_index("col")
    layer = lax.axis_index("layer")
    lead = lax.axis_index("row") ^ layer
    middle = (layer ^ (layer >> 1)) & 1
    half = here[0].shape[1]
    for s in range(4):
        panel_ref[s ^ lead] = right[s][...]
    total = None
    for s, distance in enumerate((0, 1 + middle, 2 - middle, 3)):
        for side, block in enumerate([here[s]] + there[s : s + 1]):
            rows = pl.ds(pl.multiple_of((parity ^ side) * half, half), half)
            part = jnp.dot(block[...], panel_ref[distance, rows, :], preferred_element_type=jnp.float32)
            total = part if total is None else total + part
    total_ref[...] = total
    other_ref[...] = panel_ref[3, pl.ds(pl.multiple_of((1 - parity) * half, half), half), :]


def squares_kernel(total_ref, left_ref, right_ref, weight_ref, squares_ref, sums_ref):
    product = total_ref[...] + jnp.dot(left_ref[...], right_ref[...], preferred_element_type=jnp.float32)
    squares = product * product * weight_ref[...]
    squares_ref[...] = squares
    rows, cols = squares.shape
    sums_ref[...] = jnp.sum(squares, axis=0, keepdims=True)


def scale_kernel(total_rows, squares_ref, *refs):
    sums, out_ref = refs[:-1], refs[-1]
    column = sums[0][...]
    for other in sums[1:]:
        column = column + other[...]
    column = column + epsilon
    out_ref[...] = total_rows * squares_ref[...] / column


def swap(x, axis, size, s):
    return lax.ppermute(x, axis, [(i, i ^ s) for i in range(size)])


def call(kernel, out_shape, in_specs, flops=0, size=0, **options):
    return pl.pallas_call(
        kernel,
        out_shape=out_shape,
        in_specs=in_specs,
        out_specs=jax.tree.map(lambda _: VMEM, out_shape),
        compiler_params=pltpu.CompilerParams(vmem_limit_bytes=16 * 2**20),
        cost_estimate=pl.CostEstimate(flops=flops, bytes_accessed=size, transcendentals=0),
        **options,
    )


def on_small_mesh(values, a_pattern, c_pattern, prune_mask):
    rows, cols = values.shape
    total_rows = rows * 4
    full = jax.ShapeDtypeStruct((rows, cols), jnp.float32)

    own = times_tiles(values, a_pattern.astype(jnp.float32)).astype(jnp.bfloat16)
    ring = [(0, 2), (2, 3), (3, 1), (1, 0)]
    first = lax.ppermute(own, "layer", ring)
    back = {a: b for b, a in ring}
    mixed = [
        lax.ppermute(
            own,
            ("row", "col", "layer"),
            [
                (8 * r + 4 * c + z, 8 * r + 4 * c + back[z] if c == core else 8 * (r ^ 1) + 4 * c + z)
                for r in range(4)
                for c in range(2)
                for z in range(4)
            ],
        )
        for core in range(2)
    ]
    right = [own, None] + [swap(own, "row", 4, s) for s in (2, 3)]
    weight = times_tiles(prune_mask.astype(jnp.float32), c_pattern.astype(jnp.float32))
    first, start, weight = lax.optimization_barrier((first, own, weight))
    far = lax.ppermute(first, "layer", ring)
    right[3], right[2], mixed[1], mixed[0], first, start = lax.optimization_barrier((right[3], right[2], mixed[1], mixed[0], first, start))
    first_core = lax.axis_index("col") == 0
    second = jnp.where(first_core, mixed[0], mixed[1])
    right[1] = jnp.where(first_core, mixed[1], mixed[0])
    here = [start, first, second]
    there = [swap(x, "col", 2, 1) for x in here]
    far, *there = lax.optimization_barrier((far, *there))
    far_other = swap(far, "col", 2, 1)
    total, last = call(
        most_kernel,
        [full, jax.ShapeDtypeStruct((cols, cols), jnp.bfloat16)],
        [VMEM] * 11,
        flops=2 * rows * cols * 3 * rows,
        size=2 * 10 * rows * cols,
        scratch_shapes=[pltpu.VMEM((4, rows, cols), jnp.bfloat16)],
    )(*right, *here, far, *there)
    squares, sums = call(
        squares_kernel,
        [full, jax.ShapeDtypeStruct((1, cols), jnp.float32)],
        [VMEM] * 4,
        flops=2 * rows * cols * rows,
        size=16 * rows * cols,
    )(total, far_other, last, weight)
    others = [swap(sums, "row", 4, s) for s in (1, 2, 3)]
    return call(
        functools.partial(scale_kernel, total_rows), full, [VMEM] * 5, flops=4 * rows * cols, size=8 * rows * cols
    )(squares, sums, *others)


def on_any_mesh(values, a_pattern, c_pattern, prune_mask):
    total_rows = values.shape[0] * lax.axis_size("row")
    sparse = (values * spread_tiles(a_pattern)).astype(jnp.bfloat16)
    left = lax.all_gather(sparse, ("layer", "col"), axis=1, tiled=True)
    right = lax.all_gather(sparse, "row", axis=0, tiled=True)
    kept = jnp.dot(left, right, preferred_element_type=jnp.float32) * spread_tiles(c_pattern)
    squares = kept * kept * prune_mask.astype(jnp.float32)
    column_sums = lax.psum(jnp.sum(squares, axis=0), "row")
    return total_rows * squares / (column_sums[None, :] + epsilon)


def solution(mesh):
    spec = P("row", ("layer", "col"))
    sizes = tuple(mesh.shape[name] for name in ("row", "col", "layer"))
    on_device = on_small_mesh if sizes == (4, 2, 4) else on_any_mesh
    return jax.shard_map(on_device, mesh=mesh, in_specs=(spec,) * 4, out_specs=spec, check_vma=False)
```

```python
import functools

import jax
import jax.numpy as jnp
from jax import lax
from jax.experimental import pallas as pl
from jax.experimental.pallas import tpu as pltpu
from jax.sharding import PartitionSpec as P

TILE = 128


epsilon = 1e-09

VMEM = pl.BlockSpec(memory_space=pltpu.VMEM)


def spread_tiles(pattern):
    tile_rows, tile_cols = pattern.shape
    blocked = jnp.broadcast_to(
        pattern.astype(jnp.float32)[:, None, :, None], (tile_rows, TILE, tile_cols, TILE)
    )
    return blocked.reshape(tile_rows * TILE, tile_cols * TILE)


def times_tiles(x, pattern):
    tile_rows, tile_cols = pattern.shape
    tiles = x.reshape(tile_rows, TILE, tile_cols, TILE) * pattern[:, None, :, None]
    return tiles.reshape(x.shape)


def most_kernel(*refs):
    right, here, there = refs[:4], refs[4:8], list(refs[8:11])
    total_ref, other_ref, panel_ref = refs[11:]
    parity = lax.axis_index("col")
    layer = lax.axis_index("layer")
    lead = lax.axis_index("row") ^ layer
    middle = (layer ^ (layer >> 1)) & 1
    half = here[0].shape[1]
    for s in range(4):
        panel_ref[s ^ lead] = right[s][...]
    total = None
    for s, distance in enumerate((0, 1 + middle, 2 - middle, 3)):
        for side, block in enumerate([here[s]] + there[s : s + 1]):
            rows = pl.ds(pl.multiple_of((parity ^ side) * half, half), half)
            part = jnp.dot(block[...], panel_ref[distance, rows, :], preferred_element_type=jnp.float32)
            total = part if total is None else total + part
    total_ref[...] = total
    other_ref[...] = panel_ref[3, pl.ds(pl.multiple_of((1 - parity) * half, half), half), :]


def squares_kernel(total_ref, left_ref, right_ref, weight_ref, squares_ref, sums_ref):
    product = total_ref[...] + jnp.dot(left_ref[...], right_ref[...], preferred_element_type=jnp.float32)
    squares = product * product * weight_ref[...]
    squares_ref[...] = squares
    rows, cols = squares.shape
    sums_ref[...] = jnp.sum(squares, axis=0, keepdims=True)


def scale_kernel(total_rows, squares_ref, *refs):
    sums, out_ref = refs[:-1], refs[-1]
    column = sums[0][...]
    for other in sums[1:]:
        column = column + other[...]
    column = column + epsilon
    out_ref[...] = total_rows * squares_ref[...] / column


def swap(x, axis, size, s):
    return lax.ppermute(x, axis, [(i, i ^ s) for i in range(size)])


def call(kernel, out_shape, in_specs, flops=0, size=0, **options):
    return pl.pallas_call(
        kernel,
        out_shape=out_shape,
        in_specs=in_specs,
        out_specs=jax.tree.map(lambda _: VMEM, out_shape),
        compiler_params=pltpu.CompilerParams(vmem_limit_bytes=16 * 2**20),
        cost_estimate=pl.CostEstimate(flops=flops, bytes_accessed=size, transcendentals=0),
        **options,
    )


def on_small_mesh(values, a_pattern, c_pattern, prune_mask):
    rows, cols = values.shape
    total_rows = rows * 4
    full = jax.ShapeDtypeStruct((rows, cols), jnp.float32)

    own = times_tiles(values, a_pattern.astype(jnp.float32)).astype(jnp.bfloat16)
    ring = [(0, 2), (2, 3), (3, 1), (1, 0)]
    first = lax.ppermute(own, "layer", ring)
    back = {a: b for b, a in ring}
    mixed = [
        lax.ppermute(
            own,
            ("row", "col", "layer"),
            [
                (8 * r + 4 * c + z, 8 * r + 4 * c + back[z] if c == core else 8 * (r ^ 1) + 4 * c + z)
                for r in range(4)
                for c in range(2)
                for z in range(4)
            ],
        )
        for core in range(2)
    ]
    right = [own, None] + [swap(own, "row", 4, s) for s in (2, 3)]
    weight = times_tiles(prune_mask.astype(jnp.float32), c_pattern.astype(jnp.float32))
    first, start, weight = lax.optimization_barrier((first, own, weight))
    far = lax.ppermute(first, "layer", ring)
    right[3], right[2], mixed[1], mixed[0], first, start = lax.optimization_barrier((right[3], right[2], mixed[1], mixed[0], first, start))
    first_core = lax.axis_index("col") == 0
    second = jnp.where(first_core, mixed[0], mixed[1])
    right[1] = jnp.where(first_core, mixed[1], mixed[0])
    here = [start, first, second]
    there = [swap(x, "col", 2, 1) for x in here]
    far, *there = lax.optimization_barrier((far, *there))
    far_other = swap(far, "col", 2, 1)
    total, last = call(
        most_kernel,
        [full, jax.ShapeDtypeStruct((cols, cols), jnp.bfloat16)],
        [VMEM] * 11,
        flops=2 * rows * cols * 3 * rows,
        size=2 * 10 * rows * cols,
        scratch_shapes=[pltpu.VMEM((4, rows, cols), jnp.bfloat16)],
    )(*right, *here, far, *there)
    squares, sums = call(
        squares_kernel,
        [full, jax.ShapeDtypeStruct((1, cols), jnp.float32)],
        [VMEM] * 4,
        flops=2 * rows * cols * rows,
        size=16 * rows * cols,
    )(total, far_other, last, weight)
    others = [
        lax.ppermute(sums, ("row", "col"), [(2 * r + c, 2 * (r ^ steps[c]) + c) for r in range(4) for c in range(2)])
        for steps in ((1, 3), (2, 1), (3, 2))
    ]
    return call(
        functools.partial(scale_kernel, total_rows), full, [VMEM] * 5, flops=4 * rows * cols, size=8 * rows * cols
    )(squares, sums, *others)


def on_any_mesh(values, a_pattern, c_pattern, prune_mask):
    total_rows = values.shape[0] * lax.axis_size("row")
    sparse = (values * spread_tiles(a_pattern)).astype(jnp.bfloat16)
    left = lax.all_gather(sparse, ("layer", "col"), axis=1, tiled=True)
    right = lax.all_gather(sparse, "row", axis=0, tiled=True)
    kept = jnp.dot(left, right, preferred_element_type=jnp.float32) * spread_tiles(c_pattern)
    squares = kept * kept * prune_mask.astype(jnp.float32)
    column_sums = lax.psum(jnp.sum(squares, axis=0), "row")
    return total_rows * squares / (column_sums[None, :] + epsilon)


def solution(mesh):
    spec = P("row", ("layer", "col"))
    sizes = tuple(mesh.shape[name] for name in ("row", "col", "layer"))
    on_device = on_small_mesh if sizes == (4, 2, 4) else on_any_mesh
    return jax.shard_map(on_device, mesh=mesh, in_specs=(spec,) * 4, out_specs=spec, check_vma=False)
```

```python
import functools

import jax
import jax.numpy as jnp
from jax import lax
from jax.experimental import pallas as pl
from jax.experimental.pallas import tpu as pltpu
from jax.sharding import PartitionSpec as P

TILE = 128


epsilon = 1e-09

VMEM = pl.BlockSpec(memory_space=pltpu.VMEM)


def spread_tiles(pattern):
    tile_rows, tile_cols = pattern.shape
    blocked = jnp.broadcast_to(
        pattern.astype(jnp.float32)[:, None, :, None], (tile_rows, TILE, tile_cols, TILE)
    )
    return blocked.reshape(tile_rows * TILE, tile_cols * TILE)


def times_tiles(x, pattern):
    tile_rows, tile_cols = pattern.shape
    tiles = x.reshape(tile_rows, TILE, tile_cols, TILE) * pattern[:, None, :, None]
    return tiles.reshape(x.shape)


def most_kernel(*refs):
    right, here, there = refs[:4], refs[4:8], list(refs[8:11])
    total_ref, other_ref, panel_ref = refs[11:]
    parity = lax.axis_index("col")
    layer = lax.axis_index("layer")
    lead = lax.axis_index("row") ^ layer
    middle = (layer ^ (layer >> 1)) & 1
    half = here[0].shape[1]
    for s in range(4):
        panel_ref[s ^ lead] = right[s][...]
    total = None
    for s, distance in enumerate((0, 1 + middle, 2 - middle, 3)):
        for side, block in enumerate([here[s]] + there[s : s + 1]):
            rows = pl.ds(pl.multiple_of((parity ^ side) * half, half), half)
            part = jnp.dot(block[...], panel_ref[distance, rows, :], preferred_element_type=jnp.float32)
            total = part if total is None else total + part
    total_ref[...] = total
    other_ref[...] = panel_ref[3, pl.ds(pl.multiple_of((1 - parity) * half, half), half), :]


def squares_kernel(total_ref, left_ref, right_ref, weight_ref, squares_ref, sums_ref):
    sums = None
    for i in range(total_ref.shape[0] // TILE):
        at = slice(i * TILE, (i + 1) * TILE)
        product = total_ref[at] + jnp.dot(left_ref[at], right_ref[...], preferred_element_type=jnp.float32)
        squares = product * product * weight_ref[at]
        squares_ref[at] = squares
        part = jnp.sum(squares.reshape(TILE // 8, 8, squares.shape[1]), axis=0)
        sums = part if sums is None else sums + part
    sums_ref[...] = jnp.sum(sums, axis=0, keepdims=True)


def scale_kernel(total_rows, squares_ref, *refs):
    sums, out_ref = refs[:-1], refs[-1]
    column = sums[0][...]
    for other in sums[1:]:
        column = column + other[...]
    column = column + epsilon
    out_ref[...] = total_rows * squares_ref[...] / column


def swap(x, axis, size, s):
    return lax.ppermute(x, axis, [(i, i ^ s) for i in range(size)])


def call(kernel, out_shape, in_specs, flops=0, size=0, **options):
    return pl.pallas_call(
        kernel,
        out_shape=out_shape,
        in_specs=in_specs,
        out_specs=jax.tree.map(lambda _: VMEM, out_shape),
        compiler_params=pltpu.CompilerParams(vmem_limit_bytes=16 * 2**20),
        cost_estimate=pl.CostEstimate(flops=flops, bytes_accessed=size, transcendentals=0),
        **options,
    )


def on_small_mesh(values, a_pattern, c_pattern, prune_mask):
    rows, cols = values.shape
    total_rows = rows * 4
    full = jax.ShapeDtypeStruct((rows, cols), jnp.float32)

    own = times_tiles(values, a_pattern.astype(jnp.float32)).astype(jnp.bfloat16)
    ring = [(0, 2), (2, 3), (3, 1), (1, 0)]
    first = lax.ppermute(own, "layer", ring)
    back = {a: b for b, a in ring}
    mixed = [
        lax.ppermute(
            own,
            ("row", "col", "layer"),
            [
                (8 * r + 4 * c + z, 8 * r + 4 * c + back[z] if c == core else 8 * (r ^ 1) + 4 * c + z)
                for r in range(4)
                for c in range(2)
                for z in range(4)
            ],
        )
        for core in range(2)
    ]
    right = [own, None] + [swap(own, "row", 4, s) for s in (2, 3)]
    weight = times_tiles(prune_mask.astype(jnp.float32), c_pattern.astype(jnp.float32))
    first, start, weight = lax.optimization_barrier((first, own, weight))
    far = lax.ppermute(first, "layer", ring)
    right[3], right[2], mixed[1], mixed[0], first, start = lax.optimization_barrier((right[3], right[2], mixed[1], mixed[0], first, start))
    first_core = lax.axis_index("col") == 0
    second = jnp.where(first_core, mixed[0], mixed[1])
    right[1] = jnp.where(first_core, mixed[1], mixed[0])
    here = [start, first, second]
    there = [swap(x, "col", 2, 1) for x in here]
    far, *there = lax.optimization_barrier((far, *there))
    far_other = swap(far, "col", 2, 1)
    total, last = call(
        most_kernel,
        [full, jax.ShapeDtypeStruct((cols, cols), jnp.bfloat16)],
        [VMEM] * 11,
        flops=2 * rows * cols * 3 * rows,
        size=2 * 10 * rows * cols,
        scratch_shapes=[pltpu.VMEM((4, rows, cols), jnp.bfloat16)],
    )(*right, *here, far, *there)
    squares, sums = call(
        squares_kernel,
        [full, jax.ShapeDtypeStruct((1, cols), jnp.float32)],
        [VMEM] * 4,
        flops=2 * rows * cols * rows,
        size=16 * rows * cols,
    )(total, far_other, last, weight)
    others = [swap(sums, "row", 4, s) for s in (1, 2, 3)]
    return call(
        functools.partial(scale_kernel, total_rows), full, [VMEM] * 5, flops=4 * rows * cols, size=8 * rows * cols
    )(squares, sums, *others)


def on_any_mesh(values, a_pattern, c_pattern, prune_mask):
    total_rows = values.shape[0] * lax.axis_size("row")
    sparse = (values * spread_tiles(a_pattern)).astype(jnp.bfloat16)
    left = lax.all_gather(sparse, ("layer", "col"), axis=1, tiled=True)
    right = lax.all_gather(sparse, "row", axis=0, tiled=True)
    kept = jnp.dot(left, right, preferred_element_type=jnp.float32) * spread_tiles(c_pattern)
    squares = kept * kept * prune_mask.astype(jnp.float32)
    column_sums = lax.psum(jnp.sum(squares, axis=0), "row")
    return total_rows * squares / (column_sums[None, :] + epsilon)


def solution(mesh):
    spec = P("row", ("layer", "col"))
    sizes = tuple(mesh.shape[name] for name in ("row", "col", "layer"))
    on_device = on_small_mesh if sizes == (4, 2, 4) else on_any_mesh
    return jax.shard_map(on_device, mesh=mesh, in_specs=(spec,) * 4, out_specs=spec, check_vma=False)
```
